32 devices in a mesh: tile: 8 (over z, x), mem: 4 (over y, core).
Axes of the slice: x: 2, y: 2, z: 4, core: 2. Of those that a mesh axis runs over, the one named last changes fastest.
Arguments:
- control: float32 [64, 64, 4096], P('mem', None, 'tile'), may hold values from -8 to 8
- ensemble: bfloat16 [64, 5, 64, 4096], P('mem', None, None, 'tile'), may hold values from -6 to 6
- jacobian: bfloat16 [640, 320], replicated, may hold values from -0.3125 to 0.3125
- send_columns: int32 [32, 8, 2], P(('tile', 'mem')), may hold values from 0 to 127, as said below
- received_counts: int32 [32, 8], P(('tile', 'mem')), may hold values from 0 to 2, as said below
- observed_channel: int32 [32, 8, 2, 128], P(('tile', 'mem')), may hold values from 0 to 639
- innovation: float32 [32, 8, 2, 128], P(('tile', 'mem')), may hold values from -1.5 to 1.5
- error_weight: float32 [32, 8, 2, 128], P(('tile', 'mem')), may hold values from 1 to 10
Outputs:
- gradient: float32 [64, 64, 4096], P('mem', None, 'tile')
- departures: float32 [32, 8, 2, 128], P(('tile', 'mem'))
The draws below stay inside these ranges and needn't reach their ends.
Inputs may be any that keep to these rules, and one draw needn't show every extreme that they name: `send_columns`: entry [d, t, j] is a column within the 128 columns of block k of strip s, where d = s * 4 + k; the entries of one row d are distinct. `received_counts`: entry [e, s] counts the used slots, from the first, of the 2 slots that device e receives from tile s. In each mem group one owner receives 2 from every source tile.
All inputs are finite; a program needn't handle non-finite values.
Results may differ from the reference program's by a relative error of at most 0.01.
Values may be sent and summed in bfloat16 or wider, within the bound.
A program may use at most 64 MiB of HBM per device.

```python
import math
import jax
import jax.numpy as jnp
from jax import lax

NY = 64
LV = 64
V = 5
CH = 640
NCH = 128
CAP = 2
MEMBERS = 64
MEM_GROUPS = 4
OWNERS = 8
PLACES = 32
NX = 64
TILE_COLS = 512
BLOCK_COLS = 128
NCOLS = 4096
STATE = 320


def routing_tables(key):
    base = jax.random.fold_in(key, 7)
    key_heavy, key_level, key_raw, key_perm = jax.random.split(base, 4)
    groups = PLACES // OWNERS
    heavy = jax.random.randint(key_heavy, (groups,), 0, OWNERS)
    level = jax.random.randint(key_level, (OWNERS,), 0, 4)
    raw_counts = jax.random.randint(key_raw, (PLACES, OWNERS), 0, 4)
    counts = jnp.minimum(jnp.minimum(raw_counts, level[None, :]), CAP)
    group_of = jnp.arange(PLACES) % groups
    is_heavy = jnp.arange(OWNERS)[None, :] == heavy[group_of][:, None]
    counts = jnp.where(is_heavy, CAP, counts).astype(jnp.int32)
    perm_keys = jax.random.split(key_perm, PLACES)
    perms = jax.vmap(lambda sub_key: jax.random.permutation(sub_key, BLOCK_COLS))(perm_keys)
    slot_ids = jnp.arange(OWNERS)[:, None] * CAP + jnp.arange(CAP)[None, :]
    sending = perms[:, slot_ids].astype(jnp.int32)
    received = jnp.transpose(counts.reshape(OWNERS, groups, OWNERS), (2, 1, 0)).reshape(PLACES, OWNERS)
    return (sending, received.astype(jnp.int32))


def draw_send_columns(key, part):
    return routing_tables(key)[0]


def draw_received_counts(key, part):
    return routing_tables(key)[1]


def draw_control(key, part):
    base = jax.random.fold_in(key, 11)
    key_noise, key_amplitude = jax.random.split(base, 2)
    noise = jnp.clip(jax.random.normal(key_noise, (MEMBERS, LV, NCOLS), jnp.float32), -5.0, 5.0)
    amplitude = jax.random.uniform(key_amplitude, (MEMBERS, LV, 1), jnp.float32, 2.5, 3.0)
    row_index = jnp.arange(NCOLS, dtype=jnp.int32) // NY
    row_sign = 1.0 - 2.0 * (row_index % 2).astype(jnp.float32)
    return (noise + amplitude * row_sign[None, None, :]).astype(jnp.float32)


def touch_ends(values, own_key, smallest, high):
    shape = values.shape
    index_at = [jax.random.randint(jax.random.fold_in(own_key, axis), (), 0, shape[axis]) for axis in range(len(shape))]
    values = values.at[tuple(index_at)].set(smallest)
    longest = shape.index(max(shape))
    index_at[longest] = (index_at[longest] + 1) % shape[longest]
    return values.at[tuple(index_at)].set(high)


def steps_of(own_key, shape, pieces, least, high):
    def one(axis_at, parts):
        heights = jax.random.uniform(jax.random.fold_in(jax.random.fold_in(own_key, 6), axis_at), (parts,), jnp.float32, least / len(pieces), high / len(pieces))
        return jnp.repeat(jnp.exp(heights), shape[axis_at] // parts).reshape((-1,) + (1,) * (len(shape) - axis_at - 1))

    level = one(*pieces[0])
    for cut in pieces[1:]:
        level = level * one(*cut)
    return level


def normal_values(stream_key, dims, scale, most, cuts=(), kind=jnp.bfloat16):
    entries = jax.random.normal(stream_key, dims, jnp.float32) * scale
    if len(cuts) > 0:
        entries = steps_of(stream_key, dims, cuts, -0.22, 0.18) * entries
    return jnp.clip(entries, min=-most, max=most).astype(kind)


def setup_inputs(seed: int = 0) -> dict:
    seeds = jax.random.split(jax.random.key(seed), 9)
    return {
        "control": draw_control(jax.random.fold_in(seeds[8], 71), 0),
        "ensemble": normal_values(seeds[1], (MEMBERS, V, LV, NCOLS), 1.0, 6.0, ((0, 4), (3, 8))),
        "jacobian": normal_values(seeds[2], (CH, STATE), STATE ** -0.5, 0.3125),
        "send_columns": draw_send_columns(jax.random.fold_in(seeds[8], 71), 0),
        "received_counts": draw_received_counts(jax.random.fold_in(seeds[8], 71), 0),
        "observed_channel": touch_ends(jax.random.randint(seeds[5], (PLACES, OWNERS, CAP, NCH), 0, CH), jax.random.fold_in(seeds[5], 1), 0, CH - 1).astype(jnp.int32),
        "innovation": normal_values(seeds[6], (PLACES, OWNERS, CAP, NCH), 0.25, 1.5, ((0, 32),), jnp.float32),
        "error_weight": jnp.clip(jnp.exp(math.log(10.0) - 2.3025851 * jax.random.uniform(seeds[7], (PLACES, OWNERS, CAP, NCH), jnp.float32) ** steps_of(seeds[7], (PLACES, OWNERS, CAP, NCH), ((0, 32),), -0.2, 0.2)), 1.0, 10.0),
    }


diffusion_coef = 0.2

def apply_diffusion_operator(state_field):
    padded = jnp.pad(state_field, ((0, 0), (1, 1), (1, 1)))
    beside = padded[:, 2:, 1:-1] + padded[:, :-2, 1:-1] + padded[:, 1:-1, 2:] + padded[:, 1:-1, :-2]
    return state_field + diffusion_coef * (beside - 4.0 * state_field)

def quadruple_sweeps(member_field):
    grid = member_field.reshape(LV, NX, NY)
    for sweep_turn in range(4):
        grid = apply_diffusion_operator(grid)
    return grid.reshape(LV, NCOLS)

def reference(control, ensemble, jacobian, send_columns, received_counts, observed_channel, innovation, error_weight):
    member_scale = 1.0 / math.sqrt(MEMBERS)
    localized_member_field = lax.map(quadruple_sweeps, control)
    localization_weights = localized_member_field.astype(jnp.bfloat16)

    def accumulate(carry, pair):
        weights_one, member_one = pair
        return (carry + weights_one.astype(jnp.float32)[None] * member_one.astype(jnp.float32), None)
    summed, _ = lax.scan(accumulate, jnp.zeros((V, LV, NCOLS), jnp.float32), (localization_weights, ensemble))
    increment = (summed * member_scale).astype(jnp.bfloat16).reshape(STATE, NCOLS)
    device_ids = jnp.arange(PLACES, dtype=jnp.int32)
    offsets = device_ids // MEM_GROUPS * TILE_COLS + device_ids % MEM_GROUPS * BLOCK_COLS
    carried = (offsets[:, None, None] + send_columns).astype(jnp.int32)
    columns_first = jnp.transpose(increment)
    outgoing = jnp.take(columns_first, carried.reshape(-1), axis=0)
    outgoing = outgoing.reshape(OWNERS, MEM_GROUPS, OWNERS, CAP, STATE)
    incoming = jnp.transpose(outgoing, (2, 1, 0, 3, 4)).reshape(PLACES * OWNERS * CAP, STATE)
    model_channels = jnp.dot(incoming, jnp.transpose(jacobian), preferred_element_type=jnp.float32)
    model_channels = model_channels.reshape(PLACES, OWNERS, CAP, CH)
    evolved = jnp.take_along_axis(model_channels, observed_channel, axis=3)
    filled = jnp.arange(CAP, dtype=jnp.int32)[None, None, :, None] < received_counts[:, :, None, None]
    departures = jnp.where(filled, evolved - innovation, 0.0)
    weighted = error_weight * departures
    row_count = PLACES * OWNERS * CAP
    row_ids = jnp.broadcast_to(jnp.arange(row_count, dtype=jnp.int32)[:, None], (row_count, NCH))
    channel_adjoint = jnp.zeros((row_count, CH), jnp.float32).at[row_ids, observed_channel.reshape(row_count, NCH)].add(weighted.reshape(row_count, NCH))
    channel_adjoint = channel_adjoint.astype(jnp.bfloat16)
    column_adjoint = jnp.dot(channel_adjoint, jacobian, preferred_element_type=jnp.float32).astype(jnp.bfloat16)
    returned = column_adjoint.reshape(OWNERS, MEM_GROUPS, OWNERS, CAP, STATE)
    returned = jnp.transpose(returned, (2, 1, 0, 3, 4)).reshape(row_count, STATE)
    adjoint_first = jnp.zeros((NCOLS, STATE), jnp.float32).at[carried.reshape(-1)].add(returned.astype(jnp.float32))
    analysis_increment_adjoint = jnp.transpose(adjoint_first.astype(jnp.bfloat16)).reshape(V, LV, NCOLS)

    def member_gradient(member_one):
        member_adjoint = lax.optimization_barrier(jnp.sum(member_one.astype(jnp.float32) * analysis_increment_adjoint.astype(jnp.float32), axis=0)) * member_scale
        return quadruple_sweeps(member_adjoint)
    gradient = lax.map(member_gradient, ensemble)
    return (gradient, departures)
```

```python
import math

import jax
import jax.numpy as jnp
import numpy as np
from jax import lax
from jax.sharding import PartitionSpec as P

NY = 64
SWEEPS = 4
SWEEP_SCALE = 0.2**SWEEPS


def sweep_counts(strip_rows, low_wall, high_wall):
    rows = strip_rows + 2 * SWEEPS
    field = np.zeros((strip_rows * NY, rows, NY), np.float32)
    for row in range(strip_rows):
        for y in range(NY):
            field[row * NY + y, row + SWEEPS, y] = 1.0
    inside = np.ones((rows, 1), np.float32)
    if low_wall:
        inside[:SWEEPS] = 0.0
    if high_wall:
        inside[rows - SWEEPS :] = 0.0
    for _ in range(SWEEPS):
        padded = np.pad(field, ((0, 0), (1, 1), (1, 1)))
        field = field + padded[:, 2:, 1:-1] + padded[:, :-2, 1:-1]
        field = (field + padded[:, 1:-1, 2:] + padded[:, 1:-1, :-2]) * inside
    return field.reshape(strip_rows * NY, rows * NY)


def split_two(values):
    high = lax.reduce_precision(values, 8, 7)
    return high.astype(jnp.bfloat16), (values - high).astype(jnp.bfloat16)


def dot_two(values, table, contract):
    high, low = split_two(values)
    dims = (((values.ndim - 1,), (contract,)), ((), ()))
    return SWEEP_SCALE * (
        lax.dot_general(high, table, dims, preferred_element_type=jnp.float32)
        + lax.dot_general(low, table, dims, preferred_element_type=jnp.float32)
    )


def body(
    control,
    ensemble,
    jacobian,
    send_columns,
    received_counts,
    observed_channel,
    innovation,
    error_weight,
):
    tiles = lax.axis_size("tile")
    groups = lax.axis_size("mem")
    tile_index = lax.axis_index("tile")
    members_here, levels, strip = control.shape
    variables = ensemble.shape[1]
    state = variables * levels
    member_scale = 1.0 / math.sqrt(members_here * groups)
    block = strip // groups
    owners, cap = send_columns.shape[1:]
    slots = owners * cap
    halo = SWEEPS * NY
    edge_blocks = -(-halo // block)
    edge = edge_blocks * slots
    own = groups * slots

    tables = lax.all_gather(send_columns[0].reshape(slots), ("tile", "mem"))
    tables = tables.reshape(tiles, groups, slots)
    tables = tables + (lax.iota(jnp.int32, groups) * block)[None, :, None]
    padded = jnp.pad(tables, ((1, 1), (0, 0), (0, 0)), constant_values=-4 * strip)
    near = lax.dynamic_slice_in_dim(padded, tile_index, 3, 0)
    left = near[0, groups - edge_blocks :].reshape(edge) - strip
    right = near[2, :edge_blocks].reshape(edge) + strip
    middle = near[1].reshape(own)
    carried = jnp.concatenate([left, middle, right])
    width = strip + 2 * halo
    hits = (lax.iota(jnp.int32, width)[:, None] == carried[None, :] + halo).astype(jnp.bfloat16)
    kinds = np.stack([
        sweep_counts(strip // NY, low, high) for low in (False, True) for high in (False, True)
    ]).astype(jnp.bfloat16)
    kind = 2 * (tile_index == 0).astype(jnp.int32) + (tile_index == tiles - 1).astype(jnp.int32)
    counts = lax.dynamic_index_in_dim(jnp.asarray(kinds), kind, 0, keepdims=False)
    spread = jnp.dot(counts, hits, preferred_element_type=jnp.float32).astype(jnp.bfloat16)

    partial = dot_two(control, spread, 0)
    forward = [(i, i + 1) for i in range(tiles - 1)]
    backward = [(i + 1, i) for i in range(tiles - 1)]
    from_right = lax.ppermute(partial[..., :edge], "tile", backward)
    from_left = lax.ppermute(partial[..., edge + own :], "tile", forward)
    localized = (
        partial[..., edge : edge + own]
        + jnp.pad(from_left, ((0, 0), (0, 0), (0, own - edge)))
        + jnp.pad(from_right, ((0, 0), (0, 0), (own - edge, 0)))
    )
    weights = localized.astype(jnp.bfloat16)
    own_hits = hits[halo : halo + strip, edge : edge + own]
    picked = lax.dot_general(
        ensemble, own_hits, (((3,), (0,)), ((), ())), preferred_element_type=jnp.float32
    )
    sums = jnp.sum(weights.astype(jnp.float32)[:, None] * picked, axis=0) * member_scale
    sums = jnp.transpose(sums.reshape(state, groups, owners, cap), (2, 1, 3, 0))
    parts = lax.all_to_all(
        sums.reshape(owners * groups, cap, state), ("tile", "mem"), 0, 0, tiled=True
    )
    incoming = jnp.sum(parts.reshape(owners, groups, cap, state), axis=1).astype(jnp.bfloat16)

    model = jnp.dot(
        incoming.reshape(slots, state), jnp.transpose(jacobian), preferred_element_type=jnp.float32
    )
    channels = jacobian.shape[0]
    observed = observed_channel.shape[-1]
    channel_rows = observed_channel[0].reshape(slots, observed)
    found = channel_rows[:, :, None] == lax.iota(jnp.int32, channels)[None, None, :]
    evolved = jnp.sum(jnp.where(found, model[:, None, :], 0.0), axis=2)
    evolved = evolved.reshape(owners, cap, observed)
    filled = (
        jnp.arange(cap, dtype=jnp.int32)[None, :, None] < received_counts[0][:, None, None]
    )
    departures = jnp.where(filled, evolved - innovation[0], 0.0)
    weighted = (error_weight[0] * departures).reshape(slots, observed)
    channel_adjoint = jnp.sum(jnp.where(found, weighted[:, :, None], 0.0), axis=1)
    column_adjoint = jnp.dot(
        channel_adjoint.astype(jnp.bfloat16), jacobian, preferred_element_type=jnp.float32
    ).astype(jnp.bfloat16)

    copies = jnp.broadcast_to(
        column_adjoint.reshape(owners, 1, cap, state), (owners, groups, cap, state)
    )
    returned = lax.all_to_all(
        copies.reshape(owners * groups, cap, state), ("tile", "mem"), 0, 0, tiled=True
    )
    returned = jnp.transpose(returned.reshape(owners, groups, cap, state), (3, 1, 0, 2))
    returned = returned.reshape(variables, levels, own).astype(jnp.float32)
    member_adjoint = jnp.sum(picked * returned[None], axis=1) * member_scale
    low = lax.ppermute(member_adjoint[..., own - edge :], "tile", forward)
    high = lax.ppermute(member_adjoint[..., :edge], "tile", backward)
    extended = jnp.concatenate([low, member_adjoint, high], axis=-1)
    gradient = dot_two(extended, spread, 1)
    return (gradient, departures[None])


def solution(mesh):
    in_specs = (
        P("mem", None, "tile"),
        P("mem", None, None, "tile"),
        P(),
        P(("tile", "mem"), None, None),
        P(("tile", "mem"), None),
        P(("tile", "mem"), None, None, None),
        P(("tile", "mem"), None, None, None),
        P(("tile", "mem"), None, None, None),
    )
    out_specs = (P("mem", None, "tile"), P(("tile", "mem"), None, None, None))
    return jax.shard_map(body, mesh=mesh, in_specs=in_specs, out_specs=out_specs, check_vma=False)
```

```python
import math

import jax
import jax.numpy as jnp
import numpy as np
from jax import lax
from jax.experimental import pallas as pl
from jax.experimental.pallas import tpu as pltpu
from jax.sharding import PartitionSpec as P

NY = 64
SWEEPS = 4
SWEEP_SCALE = 0.2**SWEEPS


def sweep_counts(strip_rows, low_wall, high_wall):
    rows = strip_rows + 2 * SWEEPS
    field = np.zeros((strip_rows * NY, rows, NY), np.float32)
    for row in range(strip_rows):
        for y in range(NY):
            field[row * NY + y, row + SWEEPS, y] = 1.0
    inside = np.ones((rows, 1), np.float32)
    if low_wall:
        inside[:SWEEPS] = 0.0
    if high_wall:
        inside[rows - SWEEPS :] = 0.0
    for _ in range(SWEEPS):
        padded = np.pad(field, ((0, 0), (1, 1), (1, 1)))
        field = field + padded[:, 2:, 1:-1] + padded[:, :-2, 1:-1]
        field = (field + padded[:, 1:-1, 2:] + padded[:, 1:-1, :-2]) * inside
    return field.reshape(strip_rows * NY, rows * NY)


def split_two(values):
    high = lax.reduce_precision(values, 8, 7)
    return high.astype(jnp.bfloat16), (values - high).astype(jnp.bfloat16)


def split_in_kernel(values, terms):
    pieces = []
    for _ in range(terms):
        piece = values.astype(jnp.bfloat16)
        pieces.append(piece)
        values = values - piece.astype(jnp.float32)
    return pieces


def dot(left, right, dims):
    return lax.dot_general(left, right, (dims, ((), ())), preferred_element_type=jnp.float32)


NN = ((1,), (0,))
NT = ((1,), (1,))


def kernel(
    sizes,
    table_ref,
    counts_ref,
    fold_ref,
    jacobian_ref,
    filled_ref,
    channel_ref,
    innovation_ref,
    error_ref,
    control_hbm,
    ensemble_hbm,
    extended_ref,
    spread_ref,
    departures_ref,
    control_ref,
    ensemble_ref,
    tabs,
    partial,
    halo_in,
    picked,
    sums,
    sums_in,
    rows_out,
    rows_in,
    back_out,
    back_in,
    incoming,
    channel_adjoint,
    adjoint,
    local_sem,
    table_send,
    table_recv,
    near_send,
    near_recv,
    halo_send,
    halo_recv,
    sum_send,
    sum_recv,
    there_send,
    there_recv,
    back_send,
    back_recv,
    all_send,
    all_recv,
    last_send,
    last_recv,
):
    (tiles, groups, strip, block, owners, cap, edge, members_here, levels, variables, scale) = sizes
    slots = owners * cap
    own = groups * slots
    halo = SWEEPS * NY
    state = variables * levels
    pair = 128 // levels
    pairs = members_here // pair
    tile = lax.axis_index("tile")
    mem = lax.axis_index("mem")

    control_copy = pltpu.make_async_copy(control_hbm, control_ref, local_sem.at[0])
    ensemble_copy = pltpu.make_async_copy(ensemble_hbm, ensemble_ref, local_sem.at[1])
    control_copy.start()
    ensemble_copy.start()

    def to_mem(offset):
        return {"tile": tile, "mem": lax.rem(mem + offset, groups)}

    def to_tile(offset):
        return {"tile": lax.rem(tile + offset, tiles), "mem": mem}

    def send(source, target, send_sem, recv_sem, device):
        return pltpu.make_async_remote_copy(
            src_ref=source,
            dst_ref=target,
            send_sem=send_sem,
            recv_sem=recv_sem,
            device_id=device,
            device_id_type=pl.DeviceIdType.MESH,
        )

    barrier = pltpu.get_barrier_semaphore()
    for offset in range(1, groups):
        pl.semaphore_signal(
            barrier, inc=1, device_id=to_mem(offset), device_id_type=pl.DeviceIdType.MESH
        )
    for offset in range(1, tiles):
        pl.semaphore_signal(
            barrier, inc=1, device_id=to_tile(offset), device_id_type=pl.DeviceIdType.MESH
        )
    pl.semaphore_wait(barrier, groups + tiles - 2)

    def beside(low_source, high_source, low_target, high_target, send_sem, recv_sem):
        def downward():
            device = {"tile": tile - 1, "mem": mem}
            return send(low_source, high_target, send_sem.at[0], recv_sem.at[1], device)

        def upward():
            device = {"tile": tile + 1, "mem": mem}
            return send(high_source, low_target, send_sem.at[1], recv_sem.at[0], device)

        def start():
            @pl.when(tile > 0)
            def _():
                downward().start()

            @pl.when(tile < tiles - 1)
            def _():
                upward().start()

        def wait():
            @pl.when(tile > 0)
            def _():
                downward().wait_send()
                upward().wait_recv()

            @pl.when(tile < tiles - 1)
            def _():
                upward().wait_send()
                downward().wait_recv()

        return start, wait

    def over_mem(source_of, target, send_sem, recv_sem):
        copies = [
            send(source_of(offset), target, send_sem.at[offset - 1], recv_sem.at[offset - 1],
                 to_mem(offset))
            for offset in range(1, groups)
        ]
        for copy in copies:
            copy.start()
        return copies

    def over_tile(source, target, send_sem, recv_sem):
        copies = [
            send(source.at[lax.rem(tile + offset, tiles)], target.at[tile],
                 send_sem.at[offset - 1], recv_sem.at[offset - 1], to_tile(offset))
            for offset in range(1, tiles)
        ]
        for copy in copies:
            copy.start()
        return copies

    my_rows = tabs.at[pl.ds(pl.multiple_of(edge + mem * slots, 8), slots)]
    my_rows[...] = table_ref[...]

    @pl.when(tile == 0)
    def _():
        tabs[0:edge] = jnp.full((edge, 128), -8 * strip, jnp.int32)
        halo_in[0] = jnp.zeros_like(halo_in[0])
        extended_ref[0:edge] = jnp.zeros((edge, members_here * levels), jnp.float32)

    @pl.when(tile == tiles - 1)
    def _():
        tabs[edge + own :] = jnp.full((edge, 128), 8 * strip, jnp.int32)
        halo_in[1] = jnp.zeros_like(halo_in[1])
        extended_ref[edge + own :] = jnp.zeros((edge, members_here * levels), jnp.float32)

    for copy in over_mem(lambda offset: my_rows, my_rows, table_send, table_recv):
        copy.wait()
    start, wait = beside(
        tabs.at[edge : 2 * edge], tabs.at[own : own + edge],
        tabs.at[0:edge], tabs.at[edge + own :], near_send, near_recv,
    )
    start()
    wait()

    shift = jnp.concatenate([
        jnp.full((edge, 128), halo - strip, jnp.int32),
        jnp.full((own, 128), halo, jnp.int32),
        jnp.full((edge, 128), halo + strip, jnp.int32),
    ])
    places = tabs[...] + shift
    lanes = lax.broadcasted_iota(jnp.int32, places.shape, 1)
    width = strip + 2 * halo
    hits = [
        jnp.where(places == lanes + base, 1.0, 0.0).astype(jnp.bfloat16)
        for base in range(0, width, 128)
    ]
    hits = jnp.concatenate(hits, axis=1)
    spread_ref[...] = dot(hits, counts_ref[...], NN).astype(jnp.bfloat16)

    control_copy.wait()
    chunk = 256
    for base in range(0, members_here * levels, chunk):
        high, low = split_in_kernel(control_ref[base : base + chunk], 2)
        values = dot(spread_ref[...], high, NT) + dot(spread_ref[...], low, NT)
        partial[:, base : base + chunk] = SWEEP_SCALE * values

    start, wait = beside(
        partial.at[0:edge], partial.at[edge + own :],
        halo_in.at[0], halo_in.at[1], halo_send, halo_recv,
    )
    start()
    ensemble_copy.wait()
    own_hits = hits[edge : edge + own, halo : halo + strip]
    long = pair * state
    for i in range(pairs):
        picked[i] = dot(own_hits, ensemble_ref[i * long : (i + 1) * long], NT).astype(jnp.bfloat16)
    wait()

    nothing = jnp.zeros((own - edge, 128), jnp.float32)
    total = jnp.zeros((own, long), jnp.float32)
    for i in range(pairs):
        part = slice(i * 128, (i + 1) * 128)
        localized = (
            partial[edge : edge + own, part]
            + jnp.concatenate([halo_in[0, :, part], nothing])
            + jnp.concatenate([nothing, halo_in[1, :, part]])
        )
        spread_weights = dot(localized.astype(jnp.bfloat16), fold_ref[...], NN)
        total += spread_weights * picked[i].astype(jnp.float32)
    folded = total[:, :state]
    for i in range(1, pair):
        folded = folded + total[:, i * state : (i + 1) * state]
    folded = folded * scale
    sums[:, :state] = folded

    def rows_of(offset):
        peer = lax.rem(mem + offset, groups)
        return sums.at[pl.ds(pl.multiple_of(peer * slots, 8), slots)]

    copies = over_mem(rows_of, sums_in.at[mem], sum_send, sum_recv)
    sums_in[mem] = rows_of(0)[...]
    for copy in copies:
        copy.wait()
    block_sum = jnp.sum(sums_in[...], axis=0)[:, :state]
    block_sum = block_sum.astype(jnp.bfloat16).astype(jnp.float32)
    for t in range(tiles):
        rows_out[t, :, :state] = block_sum[t * cap : (t + 1) * cap]
    copies = over_tile(rows_out, rows_in, there_send, there_recv)
    rows_in[tile] = rows_out[tile]
    for copy in copies:
        copy.wait()
    for t in range(tiles):
        incoming[t * cap : (t + 1) * cap] = rows_in[t]

    model = dot(incoming[:, :state].astype(jnp.bfloat16), jacobian_ref[...], NT)
    channels = jacobian_ref.shape[0]
    observed = channel_ref.shape[1]
    channel_adjoint[...] = model

    def observe(row, carry):
        channel = channel_ref[pl.ds(row, 1)]
        ids = lax.broadcasted_iota(jnp.int32, (channels, observed), 0)
        found = jnp.where(ids == channel, 1.0, 0.0).astype(jnp.bfloat16)
        terms = split_in_kernel(channel_adjoint[pl.ds(row, 1)], 3)
        evolved = sum(dot(term, found, NN) for term in terms)
        left = jnp.where(
            filled_ref[pl.ds(row, 1)] > 0, evolved - innovation_ref[pl.ds(row, 1)], 0.0
        )
        departures_ref[pl.ds(row, 1)] = left
        terms = split_in_kernel(left * error_ref[pl.ds(row, 1)], 3)
        channel_adjoint[pl.ds(row, 1)] = sum(dot(term, found, NT) for term in terms)
        return carry

    lax.fori_loop(0, slots, observe, 0)
    column = dot(channel_adjoint[...].astype(jnp.bfloat16), jacobian_ref[...], NN)
    column = column.astype(jnp.bfloat16).astype(jnp.float32)
    for t in range(tiles):
        back_out[t, :, :state] = column[t * cap : (t + 1) * cap]
    copies = over_tile(back_out, back_in, back_send, back_recv)
    back_in[tile] = back_out[tile]
    for copy in copies:
        copy.wait()
    for t in range(tiles):
        adjoint[mem, t * cap : (t + 1) * cap] = back_in[t]
    for copy in over_mem(
        lambda offset: adjoint.at[mem], adjoint.at[mem], all_send, all_recv
    ):
        copy.wait()

    columns = jnp.concatenate([adjoint[k][:, :state] for k in range(groups)])
    columns = jnp.concatenate([columns] * pair, axis=1)
    for i in range(pairs):
        high, low = split_in_kernel(picked[i].astype(jnp.float32) * columns, 2)
        values = dot(high, fold_ref[...], NT) + dot(low, fold_ref[...], NT)
        extended_ref[edge : edge + own, i * 128 : (i + 1) * 128] = values * scale
    start, wait = beside(
        extended_ref.at[edge : 2 * edge], extended_ref.at[own : own + edge],
        extended_ref.at[0:edge], extended_ref.at[edge + own :], last_send, last_recv,
    )
    start()
    wait()


def body(
    control,
    ensemble,
    jacobian,
    send_columns,
    received_counts,
    observed_channel,
    innovation,
    error_weight,
):
    tiles = lax.axis_size("tile")
    groups = lax.axis_size("mem")
    tile_index = lax.axis_index("tile")
    members_here, levels, strip = control.shape
    variables = ensemble.shape[1]
    state = variables * levels
    scale = 1.0 / math.sqrt(members_here * groups)
    block = strip // groups
    owners, cap = send_columns.shape[1:]
    slots = owners * cap
    halo = SWEEPS * NY
    edge = -(-halo // block) * slots
    own = groups * slots
    rows = own + 2 * edge
    long = members_here * levels
    wide = -(-state // 128) * 128
    channels = jacobian.shape[0]
    observed = observed_channel.shape[-1]
    pair = 128 // levels

    offset = lax.axis_index("mem") * block
    table = jnp.broadcast_to(send_columns[0].reshape(slots, 1) + offset, (slots, 128))
    kinds = np.stack([
        sweep_counts(strip // NY, low, high).T for low in (False, True) for high in (False, True)
    ]).astype(jnp.bfloat16)
    kind = 2 * (tile_index == 0).astype(jnp.int32) + (tile_index == tiles - 1).astype(jnp.int32)
    counts = lax.dynamic_index_in_dim(jnp.asarray(kinds), kind, 0, keepdims=False)
    fold = np.arange(pair * levels)[:, None] == (
        np.arange(pair * state) // state * levels + np.arange(pair * state) % levels
    )
    filled = jnp.arange(cap, dtype=jnp.int32)[None, :, None] < received_counts[0][:, None, None]
    filled = jnp.broadcast_to(filled, (owners, cap, observed)).astype(jnp.int32)
    sizes = (tiles, groups, strip, block, owners, cap, edge, members_here, levels, variables, scale)
    f32, bf16 = jnp.float32, jnp.bfloat16
    vmem = pl.BlockSpec(memory_space=pltpu.VMEM)
    anywhere = pl.BlockSpec(memory_space=pl.ANY)
    dma = pltpu.SemaphoreType.DMA
    extended, spread, departures = pl.pallas_call(
        lambda *refs: kernel(sizes, *refs),
        out_shape=(
            jax.ShapeDtypeStruct((rows, long), f32),
            jax.ShapeDtypeStruct((rows, strip), bf16),
            jax.ShapeDtypeStruct((slots, observed), f32),
        ),
        in_specs=[vmem] * 8 + [anywhere] * 2,
        out_specs=(vmem, vmem, vmem),
        scratch_shapes=[
            pltpu.VMEM((long, strip), f32),
            pltpu.VMEM((long * variables, strip), bf16),
            pltpu.VMEM((rows, 128), jnp.int32),
            pltpu.VMEM((rows, long), f32),
            pltpu.VMEM((2, edge, long), f32),
            pltpu.VMEM((members_here // pair, own, pair * state), bf16),
            pltpu.VMEM((own, wide), f32),
            pltpu.VMEM((groups, slots, wide), f32),
            pltpu.VMEM((tiles, cap, wide), f32),
            pltpu.VMEM((tiles, cap, wide), f32),
            pltpu.VMEM((tiles, cap, wide), f32),
            pltpu.VMEM((tiles, cap, wide), f32),
            pltpu.VMEM((slots, wide), f32),
            pltpu.VMEM((slots, channels), f32),
            pltpu.VMEM((groups, slots, wide), f32),
            dma((2,)),
            dma((groups,)), dma((groups,)),
            dma((2,)), dma((2,)),
            dma((2,)), dma((2,)),
            dma((groups,)), dma((groups,)),
            dma((tiles,)), dma((tiles,)),
            dma((tiles,)), dma((tiles,)),
            dma((groups,)), dma((groups,)),
            dma((2,)), dma((2,)),
        ],
        compiler_params=pltpu.CompilerParams(
            collective_id=0, has_side_effects=True, vmem_limit_bytes=48 * 1024 * 1024
        ),
    )(
        table,
        counts,
        jnp.asarray(fold, bf16),
        jacobian,
        filled.reshape(slots, observed),
        observed_channel[0].reshape(slots, observed),
        innovation[0].reshape(slots, observed),
        error_weight[0].reshape(slots, observed),
        control.reshape(long, strip),
        ensemble.reshape(long * variables, strip),
    )
    high, low = split_two(extended)
    gradient = SWEEP_SCALE * (dot(high, spread, ((0,), (0,))) + dot(low, spread, ((0,), (0,))))
    departures = departures.reshape(1, owners, cap, observed)
    return (gradient.reshape(control.shape), departures)


def solution(mesh):
    in_specs = (
        P("mem", None, "tile"),
        P("mem", None, None, "tile"),
        P(),
        P(("tile", "mem"), None, None),
        P(("tile", "mem"), None),
        P(("tile", "mem"), None, None, None),
        P(("tile", "mem"), None, None, None),
        P(("tile", "mem"), None, None, None),
    )
    out_specs = (P("mem", None, "tile"), P(("tile", "mem"), None, None, None))
    return jax.shard_map(body, mesh=mesh, in_specs=in_specs, out_specs=out_specs, check_vma=False)
```

```python
import math

import jax
import jax.numpy as jnp
import numpy as np
from jax import lax
from jax.experimental import pallas as pl
from jax.experimental.pallas import tpu as pltpu
from jax.sharding import PartitionSpec as P

NY = 64
SWEEPS = 4
SWEEP_SCALE = 0.2**SWEEPS


def sweep_counts(strip_rows, low_wall, high_wall):
    rows = strip_rows + 2 * SWEEPS
    field = np.zeros((strip_rows * NY, rows, NY), np.float32)
    for row in range(strip_rows):
        for y in range(NY):
            field[row * NY + y, row + SWEEPS, y] = 1.0
    inside = np.ones((rows, 1), np.float32)
    if low_wall:
        inside[:SWEEPS] = 0.0
    if high_wall:
        inside[rows - SWEEPS :] = 0.0
    for _ in range(SWEEPS):
        padded = np.pad(field, ((0, 0), (1, 1), (1, 1)))
        field = field + padded[:, 2:, 1:-1] + padded[:, :-2, 1:-1]
        field = (field + padded[:, 1:-1, 2:] + padded[:, 1:-1, :-2]) * inside
    return field.reshape(strip_rows * NY, rows * NY)


def split_in_kernel(values, terms):
    pieces = []
    for _ in range(terms):
        piece = values.astype(jnp.bfloat16)
        pieces.append(piece)
        values = values - piece.astype(jnp.float32)
    return pieces


def dot(left, right, dims):
    return lax.dot_general(left, right, (dims, ((), ())), preferred_element_type=jnp.float32)


NN = ((1,), (0,))
NT = ((1,), (1,))


def kernel(
    sizes,
    table_ref,
    fold_ref,
    channel_ref,
    innovation_ref,
    error_ref,
    control_hbm,
    ensemble_hbm,
    counts_hbm,
    jacobian_hbm,
    extended_ref,
    spread_ref,
    departures_ref,
    control_ref,
    ensemble_ref,
    counts_ref,
    jacobian_ref,
    found_ref,
    tabs,
    partial,
    halo_out,
    halo_in,
    picked,
    sums,
    sums_in,
    rows_out,
    rows_in,
    back_out,
    back_in,
    incoming,
    channel_adjoint,
    adjoint,
    local_sem,
    table_send,
    table_recv,
    near_send,
    near_recv,
    halo_send,
    halo_recv,
    sum_send,
    sum_recv,
    there_send,
    there_recv,
    back_send,
    back_recv,
    all_send,
    all_recv,
    last_send,
    last_recv,
):
    (tiles, groups, strip, block, owners, cap, edge, members_here, levels, variables, scale) = sizes
    slots = owners * cap
    own = groups * slots
    halo = SWEEPS * NY
    state = variables * levels
    pair = 128 // levels
    pairs = members_here // pair
    tile = lax.axis_index("tile")
    mem = lax.axis_index("mem")

    control_copy = pltpu.make_async_copy(control_hbm, control_ref, local_sem.at[0])
    ensemble_copy = pltpu.make_async_copy(ensemble_hbm, ensemble_ref, local_sem.at[1])
    kind = jnp.where(tile == 0, 2, 0) + jnp.where(tile == tiles - 1, 1, 0)
    counts_copy = pltpu.make_async_copy(counts_hbm.at[kind], counts_ref, local_sem.at[2])
    jacobian_copy = pltpu.make_async_copy(jacobian_hbm, jacobian_ref, local_sem.at[3])
    counts_copy.start()
    control_copy.start()
    ensemble_copy.start()
    jacobian_copy.start()

    def to_mem(offset):
        return {"tile": tile, "mem": lax.rem(mem + offset, groups)}

    def to_tile(offset):
        return {"tile": lax.rem(tile + offset, tiles), "mem": mem}

    def send(source, target, send_sem, recv_sem, device):
        return pltpu.make_async_remote_copy(
            src_ref=source,
            dst_ref=target,
            send_sem=send_sem,
            recv_sem=recv_sem,
            device_id=device,
            device_id_type=pl.DeviceIdType.MESH,
        )

    barrier = pltpu.get_barrier_semaphore()
    for offset in range(1, groups):
        pl.semaphore_signal(
            barrier, inc=1, device_id=to_mem(offset), device_id_type=pl.DeviceIdType.MESH
        )
    for offset in range(1, tiles):
        pl.semaphore_signal(
            barrier, inc=1, device_id=to_tile(offset), device_id_type=pl.DeviceIdType.MESH
        )
    pl.semaphore_wait(barrier, groups + tiles - 2)

    def beside(low_source, high_source, low_target, high_target, send_sem, recv_sem):
        def downward():
            device = {"tile": tile - 1, "mem": mem}
            return send(low_source, high_target, send_sem.at[0], recv_sem.at[1], device)

        def upward():
            device = {"tile": tile + 1, "mem": mem}
            return send(high_source, low_target, send_sem.at[1], recv_sem.at[0], device)

        def start():
            @pl.when(tile > 0)
            def _():
                downward().start()

            @pl.when(tile < tiles - 1)
            def _():
                upward().start()

        def wait():
            @pl.when(tile > 0)
            def _():
                downward().wait_send()
                upward().wait_recv()

            @pl.when(tile < tiles - 1)
            def _():
                upward().wait_send()
                downward().wait_recv()

        return start, wait

    def over_mem(source_of, target, send_sem, recv_sem):
        copies = [
            send(source_of(offset), target, send_sem.at[offset - 1], recv_sem.at[offset - 1],
                 to_mem(offset))
            for offset in range(1, groups)
        ]
        for copy in copies:
            copy.start()
        return copies

    def over_tile(source, target, send_sem, recv_sem):
        copies = [
            send(source.at[lax.rem(tile + offset, tiles)], target.at[tile],
                 send_sem.at[offset - 1], recv_sem.at[offset - 1], to_tile(offset))
            for offset in range(1, tiles)
        ]
        for copy in copies:
            copy.start()
        return copies

    my_rows = tabs.at[pl.ds(pl.multiple_of(edge + mem * slots, 8), slots)]
    my_rows[...] = table_ref[0:slots]

    @pl.when(tile == 0)
    def _():
        tabs[0:edge] = jnp.full((edge, 128), -8 * strip, jnp.int32)
        halo_in[0] = jnp.zeros_like(halo_in[0])
        extended_ref[0:edge] = jnp.zeros((edge, members_here * levels), jnp.bfloat16)

    @pl.when(tile == tiles - 1)
    def _():
        tabs[edge + own :] = jnp.full((edge, 128), 8 * strip, jnp.int32)
        halo_in[1] = jnp.zeros_like(halo_in[1])
        extended_ref[edge + own :] = jnp.zeros((edge, members_here * levels), jnp.bfloat16)

    for copy in over_mem(lambda offset: my_rows, my_rows, table_send, table_recv):
        copy.wait()
    start, wait = beside(
        tabs.at[edge : 2 * edge], tabs.at[own : own + edge],
        tabs.at[0:edge], tabs.at[edge + own :], near_send, near_recv,
    )
    start()
    wait()

    shift = jnp.concatenate([
        jnp.full((edge, 128), halo - strip, jnp.int32),
        jnp.full((own, 128), halo, jnp.int32),
        jnp.full((edge, 128), halo + strip, jnp.int32),
    ])
    places = tabs[...] + shift
    lanes = lax.broadcasted_iota(jnp.int32, places.shape, 1)
    width = strip + 2 * halo
    hits = [
        jnp.where(places == lanes + base, 1.0, 0.0).astype(jnp.bfloat16)
        for base in range(0, width, 128)
    ]
    hits = jnp.concatenate(hits, axis=1)
    counts_copy.wait()
    spread_ref[...] = dot(hits, counts_ref[...], NN).astype(jnp.bfloat16)

    control_copy.wait()
    chunk = 256
    for base in range(0, members_here * levels, chunk):
        high, low = split_in_kernel(control_ref[base : base + chunk], 2)
        values = dot(spread_ref[...], high, NT) + dot(spread_ref[...], low, NT)
        partial[:, base : base + chunk] = SWEEP_SCALE * values

    halo_out[0] = partial[0:edge].astype(jnp.bfloat16)
    halo_out[1] = partial[edge + own :].astype(jnp.bfloat16)
    start, wait = beside(
        halo_out.at[0], halo_out.at[1],
        halo_in.at[0], halo_in.at[1], halo_send, halo_recv,
    )
    start()
    ensemble_copy.wait()
    own_hits = hits[edge : edge + own, halo : halo + strip]
    long = pair * state
    for i in range(pairs):
        picked[i] = dot(own_hits, ensemble_ref[i * long : (i + 1) * long], NT).astype(jnp.bfloat16)
    channels = jacobian_ref.shape[1]
    observed = channel_ref.shape[1]

    def find(row, carry):
        ids = lax.broadcasted_iota(jnp.int32, (channels, observed), 0)
        hit = ids == channel_ref[pl.ds(row, 1)]
        found_ref[row] = jnp.where(hit, 1.0, 0.0).astype(jnp.bfloat16)
        return carry

    lax.fori_loop(0, slots, find, 0)
    jacobian_copy.wait()
    wait()

    nothing = jnp.zeros((own - edge, 128), jnp.float32)
    total = jnp.zeros((own, long), jnp.float32)
    for i in range(pairs):
        part = slice(i * 128, (i + 1) * 128)
        localized = (
            partial[edge : edge + own, part]
            + jnp.concatenate([halo_in[0, :, part].astype(jnp.float32), nothing])
            + jnp.concatenate([nothing, halo_in[1, :, part].astype(jnp.float32)])
        )
        spread_weights = dot(localized.astype(jnp.bfloat16), fold_ref[...], NN)
        total += spread_weights * picked[i].astype(jnp.float32)
    folded = total[:, :state]
    for i in range(1, pair):
        folded = folded + total[:, i * state : (i + 1) * state]
    folded = folded * scale
    sums[:, :state] = folded

    def rows_of(offset):
        peer = lax.rem(mem + offset, groups)
        return sums.at[pl.ds(pl.multiple_of(peer * slots, 8), slots)]

    copies = over_mem(rows_of, sums_in.at[mem], sum_send, sum_recv)
    sums_in[mem] = rows_of(0)[...]
    for copy in copies:
        copy.wait()
    block_sum = jnp.sum(sums_in[...], axis=0)[:, :state]
    block_sum = block_sum.astype(jnp.bfloat16).astype(jnp.float32)
    for t in range(tiles):
        rows_out[t, :, :state] = block_sum[t * cap : (t + 1) * cap]
    copies = over_tile(rows_out, rows_in, there_send, there_recv)
    rows_in[tile] = rows_out[tile]
    for copy in copies:
        copy.wait()
    for t in range(tiles):
        incoming[t * cap : (t + 1) * cap] = rows_in[t]

    model = dot(incoming[:, :state].astype(jnp.bfloat16), jacobian_ref[...], NN)
    channel_adjoint[...] = model

    def stacked(values):
        terms = [term.astype(jnp.float32) for term in split_in_kernel(values, 3)]
        blank = jnp.zeros((5, values.shape[1]), jnp.float32)
        return jnp.concatenate(terms + [blank]).astype(jnp.bfloat16)

    def observe(row, carry):
        found = found_ref[row]
        evolved = dot(stacked(channel_adjoint[pl.ds(row, 1)]), found, NN)
        evolved = jnp.sum(evolved, axis=0, keepdims=True)
        left = jnp.where(
            table_ref[pl.ds(slots + row, 1)] > 0, evolved - innovation_ref[pl.ds(row, 1)], 0.0
        )
        departures_ref[pl.ds(row, 1)] = left
        adjoint_terms = dot(stacked(left * error_ref[pl.ds(row, 1)]), found, NT)
        channel_adjoint[pl.ds(row, 1)] = jnp.sum(adjoint_terms, axis=0, keepdims=True)
        return carry

    lax.fori_loop(0, slots, observe, 0, unroll=math.gcd(slots, 16))
    column = dot(channel_adjoint[...].astype(jnp.bfloat16), jacobian_ref[...], NT)
    column = column.astype(jnp.bfloat16).astype(jnp.float32)
    for t in range(tiles):
        back_out[t, :, :state] = column[t * cap : (t + 1) * cap]
    copies = over_tile(back_out, back_in, back_send, back_recv)
    back_in[tile] = back_out[tile]
    for copy in copies:
        copy.wait()
    for t in range(tiles):
        adjoint[mem, t * cap : (t + 1) * cap] = back_in[t]
    for copy in over_mem(
        lambda offset: adjoint.at[mem], adjoint.at[mem], all_send, all_recv
    ):
        copy.wait()

    columns = jnp.concatenate([adjoint[k][:, :state] for k in range(groups)])
    columns = jnp.concatenate([columns] * pair, axis=1)
    for i in range(pairs):
        high, low = split_in_kernel(picked[i].astype(jnp.float32) * columns, 2)
        values = dot(high, fold_ref[...], NT) + dot(low, fold_ref[...], NT)
        extended_ref[edge : edge + own, i * 128 : (i + 1) * 128] = (values * scale).astype(jnp.bfloat16)
    start, wait = beside(
        extended_ref.at[edge : 2 * edge], extended_ref.at[own : own + edge],
        extended_ref.at[0:edge], extended_ref.at[edge + own :], last_send, last_recv,
    )
    start()
    wait()


def body(
    control,
    ensemble,
    jacobian,
    send_columns,
    received_counts,
    observed_channel,
    innovation,
    error_weight,
):
    tiles = lax.axis_size("tile")
    groups = lax.axis_size("mem")
    members_here, levels, strip = control.shape
    variables = ensemble.shape[1]
    state = variables * levels
    scale = 1.0 / math.sqrt(members_here * groups)
    block = strip // groups
    owners, cap = send_columns.shape[1:]
    slots = owners * cap
    halo = SWEEPS * NY
    edge = -(-halo // block) * slots
    own = groups * slots
    rows = own + 2 * edge
    long = members_here * levels
    wide = -(-state // 128) * 128
    channels = jacobian.shape[0]
    observed = observed_channel.shape[-1]
    pair = 128 // levels

    offset = lax.axis_index("mem") * block
    table = jnp.broadcast_to(send_columns[0].reshape(slots, 1) + offset, (slots, 128))
    kinds = np.stack([
        sweep_counts(strip // NY, low, high).T for low in (False, True) for high in (False, True)
    ]).astype(jnp.bfloat16)
    fold = np.arange(pair * levels)[:, None] == (
        np.arange(pair * state) // state * levels + np.arange(pair * state) % levels
    )
    filled = jnp.arange(cap, dtype=jnp.int32)[None, :, None] < received_counts[0][:, None, None]
    filled = jnp.broadcast_to(filled, (owners, cap, 128)).astype(jnp.int32)
    table = jnp.concatenate([table, filled.reshape(slots, 128)])
    sizes = (tiles, groups, strip, block, owners, cap, edge, members_here, levels, variables, scale)
    f32, bf16 = jnp.float32, jnp.bfloat16
    vmem = pl.BlockSpec(memory_space=pltpu.VMEM)
    anywhere = pl.BlockSpec(memory_space=pl.ANY)
    dma = pltpu.SemaphoreType.DMA
    extended, spread, departures = pl.pallas_call(
        lambda *refs: kernel(sizes, *refs),
        out_shape=(
            jax.ShapeDtypeStruct((rows, long), bf16),
            jax.ShapeDtypeStruct((rows, strip), bf16),
            jax.ShapeDtypeStruct((slots, observed), f32),
        ),
        in_specs=[vmem] * 5 + [anywhere] * 4,
        out_specs=(vmem, vmem, vmem),
        scratch_shapes=[
            pltpu.VMEM((long, strip), f32),
            pltpu.VMEM((long * variables, strip), bf16),
            pltpu.VMEM(kinds.shape[1:], bf16),
            pltpu.VMEM((state, channels), bf16),
            pltpu.VMEM((slots, channels, observed), bf16),
            pltpu.VMEM((rows, 128), jnp.int32),
            pltpu.VMEM((rows, long), f32),
            pltpu.VMEM((2, edge, long), bf16),
            pltpu.VMEM((2, edge, long), bf16),
            pltpu.VMEM((members_here // pair, own, pair * state), bf16),
            pltpu.VMEM((own, wide), f32),
            pltpu.VMEM((groups, slots, wide), f32),
            pltpu.VMEM((tiles, cap, wide), f32),
            pltpu.VMEM((tiles, cap, wide), f32),
            pltpu.VMEM((tiles, cap, wide), f32),
            pltpu.VMEM((tiles, cap, wide), f32),
            pltpu.VMEM((slots, wide), f32),
            pltpu.VMEM((slots, channels), f32),
            pltpu.VMEM((groups, slots, wide), f32),
            dma((4,)),
            dma((groups,)), dma((groups,)),
            dma((2,)), dma((2,)),
            dma((2,)), dma((2,)),
            dma((groups,)), dma((groups,)),
            dma((tiles,)), dma((tiles,)),
            dma((tiles,)), dma((tiles,)),
            dma((groups,)), dma((groups,)),
            dma((2,)), dma((2,)),
        ],
        compiler_params=pltpu.CompilerParams(
            collective_id=0, has_side_effects=True, vmem_limit_bytes=48 * 1024 * 1024
        ),
    )(
        table,
        jnp.asarray(fold, bf16),
        observed_channel[0].reshape(slots, observed),
        innovation[0].reshape(slots, observed),
        error_weight[0].reshape(slots, observed),
        control.reshape(long, strip),
        ensemble.reshape(long * variables, strip),
        jnp.asarray(kinds),
        jnp.transpose(jacobian),
    )
    gradient = SWEEP_SCALE * dot(extended, spread, ((0,), (0,)))
    departures = departures.reshape(1, owners, cap, observed)
    return (gradient.reshape(control.shape), departures)


def solution(mesh):
    in_specs = (
        P("mem", None, "tile"),
        P("mem", None, None, "tile"),
        P(),
        P(("tile", "mem"), None, None),
        P(("tile", "mem"), None),
        P(("tile", "mem"), None, None, None),
        P(("tile", "mem"), None, None, None),
        P(("tile", "mem"), None, None, None),
    )
    out_specs = (P("mem", None, "tile"), P(("tile", "mem"), None, None, None))
    return jax.shard_map(body, mesh=mesh, in_specs=in_specs, out_specs=out_specs, check_vma=False)
```
